32 devices in a mesh: tok: 8 (over z, x), head: 4 (over y, core).
Axes of the slice: x: 2, y: 2, z: 4, core: 2. Of those that a mesh axis runs over, the one named last changes fastest.
Arguments:
- queries: bfloat16 [3072, 4096], P('tok', 'head'), may hold values from -100 to 100
- keys: bfloat16 [3072, 1024], P('tok', 'head'), may hold values from -5 to 5
- values: bfloat16 [3072, 1024], P('tok', 'head'), may hold values from -6 to 6
- lengths: int32 [16], replicated, may hold values from 1 to 1536, 3072 in all
- out_weight: bfloat16 [4096, 4096], P('head', 'tok'), may hold values from -0.09375 to 0.09375
Outputs:
- mixed: bfloat16 [3072, 4096], P('tok', 'head')
The draws below stay inside these ranges and needn't reach their ends.
Inputs may be any that keep to these rules, and one draw needn't show every extreme that they name: Every document has at most 1536 tokens and the lengths sum to 3072.
All inputs are finite; a program needn't handle non-finite values.
Results may differ from the reference program's by a relative error of at most 0.015.
Values may be sent and summed in bfloat16 or wider, within the bound.
No kernel may reach another device: no remote copies, remote signals or barrier semaphores. Data moves between devices by JAX's collectives and lax.ppermute only.
A program may use at most 64 MiB of HBM per device.

```python
import math
import jax
import jax.numpy as jnp
import numpy as np
from jax import lax

D = 4096
QH = 32
KVH = 8
HD = 128
DOCS = 16
TOKENS = 3072
MOST = 1536


def shared_keys(key):
    base = jax.random.normal(jax.random.fold_in(key, 7), (TOKENS, KVH * HD), jnp.float32)
    base = jnp.clip(base, -5.0, 5.0)
    return base


def draw_keys(key, part):
    return shared_keys(key).astype(jnp.bfloat16)


def draw_queries(key, part):
    fresh = jax.random.normal(jax.random.fold_in(key, 11), (TOKENS, QH * HD), jnp.float32)
    fresh = jnp.clip(fresh, -6.0, 6.0)
    return fresh.astype(jnp.bfloat16)


def levels(rng, extent, pieces, low, top_value):
    factor_of, own = 1.0, jax.random.fold_in(rng, 6)
    for dim, shards_of in pieces:
        heights = jnp.exp(jax.random.uniform(jax.random.fold_in(own, dim), (shards_of,), jnp.float32, low / len(pieces), top_value / len(pieces)))
        factor_of = factor_of * jnp.repeat(heights, extent[dim] // shards_of).reshape([-1 if axis == dim else 1 for axis in range(len(extent))])
    return factor_of


def length_profile(count, total, reach, lean):
    portions = [(1 << 20) // math.isqrt(grade ** lean) + 1 for grade in range(2, count + 1)]
    rest, given = total - reach - (count - 1), [1] * (count - 1)
    while rest > 0:
        movable = [i for i in range(count - 1) if given[i] < reach]
        pool, budget = sum([portions[i] for i in movable]), rest
        for i in movable:
            more = min(reach - given[i], max(1, budget * portions[i] // pool), rest)
            given[i] = given[i] + more
            rest = rest - more
    return np.array([reach] + given)


def uneven(stream_key, amount, total, bound, skew):
    if amount == 2:
        one = jax.random.randint(stream_key, (), max(1, total - bound), min(bound, total - 1) + 1)
        return jnp.stack([one, total - one])
    sizes = jnp.asarray(length_profile(amount, total, bound, skew), jnp.int32)
    couples = (amount - 1) // 2
    donor, taker = sizes[1:1 + 2 * couples:2], sizes[2:2 + 2 * couples:2]
    room = jnp.minimum(donor - 1, bound - taker)
    moved = jax.random.randint(jax.random.fold_in(stream_key, 1), (couples,), 0, 1 << 20) % (room + 1)
    sizes = sizes.at[1:1 + 2 * couples:2].set(donor - moved).at[2:2 + 2 * couples:2].set(taker + moved)
    return sizes[jax.random.permutation(jax.random.fold_in(stream_key, 2), amount)]


def bell_draw(own_key, extent, scale, most, cuts=(), kind=jnp.bfloat16):
    drawn = scale * jax.random.normal(own_key, extent, jnp.float32)
    if cuts:
        drawn = drawn * levels(own_key, extent, cuts, -0.22, 0.18)
    return jnp.clip(drawn, -most, most).astype(kind)


def setup_inputs(seed: int = 0) -> dict:
    splits = jax.random.split(jax.random.key(seed), 6)
    return {
        "queries": draw_queries(jax.random.fold_in(splits[5], 71), 0),
        "keys": draw_keys(jax.random.fold_in(splits[5], 71), 0),
        "values": bell_draw(splits[2], (TOKENS, KVH * HD), 1.0, 6.0, ((0, 8), (1, 4))),
        "lengths": uneven(splits[3], DOCS, TOKENS, MOST, 2).astype(jnp.int32),
        "out_weight": bell_draw(splits[4], (QH * HD, D), (QH * HD) ** -0.5, 0.09375, ((0, 4), (1, 8))),
    }


def doc_index(lengths, positions):
    ends = jnp.cumsum(lengths)
    return jnp.sum((positions[:, None] >= ends[None, :]).astype(jnp.int32), axis=1).astype(jnp.int32)


def reference(queries, keys, values, lengths, out_weight):
    ratio = QH // KVH
    block = min(512, TOKENS)
    nblocks = TOKENS // block
    scale = 1.0 / (HD ** 0.5)
    positions = jnp.arange(TOKENS, dtype=jnp.int32)
    docs = doc_index(lengths, positions)
    qall = queries.reshape(TOKENS, KVH, ratio, HD)
    kall = keys.reshape(TOKENS, KVH, HD)
    vall = values.reshape(TOKENS, KVH, HD)

    def one_block(index):
        group = index // nblocks
        start = (index % nblocks) * block
        qblock = lax.dynamic_slice_in_dim(qall, start, block, 0)
        qblock = lax.dynamic_index_in_dim(qblock, group, 1, keepdims=False)
        kgroup = lax.dynamic_index_in_dim(kall, group, 1, keepdims=False)
        vgroup = lax.dynamic_index_in_dim(vall, group, 1, keepdims=False)
        scores = jnp.einsum("qrd,kd->rqk", qblock.astype(jnp.float32), kgroup.astype(jnp.float32)) * scale
        qpos = start + jnp.arange(block, dtype=jnp.int32)
        qdoc = lax.dynamic_slice_in_dim(docs, start, block, 0)
        allowed = (qdoc[:, None] == docs[None, :]) & (positions[None, :] <= qpos[:, None])
        scores = jnp.where(allowed[None], scores, jnp.float32(-1e30))
        top = jnp.max(scores, axis=-1, keepdims=True)
        weights = jnp.where(allowed[None], jnp.exp(scores - top), jnp.float32(0.0))
        total = jnp.sum(weights, axis=-1)
        low = weights.astype(jnp.bfloat16)
        summed = jnp.einsum("rqk,kd->rqd", low.astype(jnp.float32), vgroup.astype(jnp.float32))
        result = summed / total[..., None]
        return jnp.transpose(result, (1, 0, 2))

    outs = lax.map(one_block, jnp.arange(KVH * nblocks, dtype=jnp.int32))
    outs = outs.reshape(KVH, nblocks, block, ratio, HD)
    outs = jnp.transpose(outs, (1, 2, 0, 3, 4)).reshape(TOKENS, QH * HD)
    attn = outs.astype(jnp.bfloat16)
    return jnp.dot(attn, out_weight, preferred_element_type=jnp.float32).astype(jnp.bfloat16)
```

```python
import functools
import math

import jax
import jax.numpy as jnp
from jax import lax
from jax.experimental import pallas as pl
from jax.experimental.pallas import tpu as pltpu
from jax.sharding import PartitionSpec as P

QH = 32
KVH = 8
HD = 128
RATIO = QH // KVH
SCALE = 1.0 / HD**0.5
LOW = -1e30


def doc_ends(lengths):
    order = jnp.arange(lengths.shape[0], dtype=jnp.int32)
    return jnp.sum(jnp.where(order[None, :] <= order[:, None], lengths[None, :], 0), axis=1)


def doc_starts(lengths, positions):
    ends = doc_ends(lengths)[None, :]
    return jnp.max(jnp.where(ends <= positions[:, None], ends, 0), axis=1)


def attend_kernel(count, own, resume, last, bases, q_ref, start_ref, *refs):
    keys, vals = refs[:count], refs[count : 2 * count]
    refs = refs[2 * count :]
    if resume:
        acc_in, top_in = refs[:2]
        refs = refs[2:]
    query = q_ref[...]
    start = start_ref[...]
    rows = query.shape[0]
    factor = SCALE * math.log2(math.e)
    scores = []
    top = top_in[:, :1] if resume else None
    for i in range(count):
        s = lax.dot_general(
            query, keys[i][...], (((1,), (1,)), ((), ())), preferred_element_type=jnp.float32
        )
        column = lax.broadcasted_iota(jnp.int32, s.shape, 1)
        allowed = column >= start - bases[i]
        if own and i == 0:
            allowed = allowed & (column <= lax.broadcasted_iota(jnp.int32, s.shape, 0))
        s = jnp.where(allowed, s, LOW)
        high = jnp.max(s, axis=1, keepdims=True)
        top = high if top is None else jnp.maximum(top, high)
        scores.append(s)
    acc = None
    for i in range(count):
        weights = jnp.exp2((scores[i] - top) * factor).astype(jnp.bfloat16)
        value = vals[i][...]
        wide = jnp.concatenate([value, jnp.ones_like(value)], axis=1)
        part = jnp.dot(weights, wide, preferred_element_type=jnp.float32)
        acc = part if acc is None else acc + part
    if resume:
        acc = acc + acc_in[...] * jnp.exp2((top_in[:, :1] - top) * factor)
    if last:
        out_ref = refs[0]
        out_ref[...] = (acc[:, :HD] / acc[:, HD:]).astype(out_ref.dtype)
    else:
        acc_out, top_out = refs
        acc_out[...] = acc
        top_out[...] = jnp.broadcast_to(top, (rows, HD))


def attend(queries, start, pieces, bases, own, state, last):
    rows, width = queries.shape
    heads = width // HD
    groups = heads // RATIO
    count = len(pieces)
    resume = state is not None
    specs = [
        pl.BlockSpec((rows, HD), lambda h, b: (0, h)),
        pl.BlockSpec((rows, 1), lambda h, b: (0, 0)),
    ]
    specs += [pl.BlockSpec((p.shape[0], HD), lambda h, b: (0, h // RATIO)) for p in pieces]
    specs += [
        pl.BlockSpec((p.shape[0], HD), lambda h, b, g=groups: (0, g + h // RATIO)) for p in pieces
    ]
    state_specs = [
        pl.BlockSpec((rows, 2 * HD), lambda h, b: (0, h)),
        pl.BlockSpec((rows, HD), lambda h, b: (0, h)),
    ]
    if resume:
        specs += state_specs
    if last:
        out_shape = jax.ShapeDtypeStruct((rows, width), jnp.bfloat16)
        out_specs = pl.BlockSpec((rows, HD), lambda h, b: (0, h))
    else:
        out_shape = (
            jax.ShapeDtypeStruct((rows, 2 * width), jnp.float32),
            jax.ShapeDtypeStruct((rows, width), jnp.float32),
        )
        out_specs = tuple(state_specs)
    seen = sum(p.shape[0] for p in pieces)
    return pl.pallas_call(
        functools.partial(attend_kernel, count, own, resume, last),
        grid_spec=pltpu.PrefetchScalarGridSpec(
            num_scalar_prefetch=1,
            grid=(heads,),
            in_specs=specs,
            out_specs=out_specs,
        ),
        out_shape=out_shape,
        compiler_params=pltpu.CompilerParams(vmem_limit_bytes=40 * 2**20),
        cost_estimate=pl.CostEstimate(
            flops=6 * rows * seen * width,
            bytes_accessed=4 * rows * width,
            transcendentals=rows * seen * heads,
        ),
    )(bases, queries, start, *pieces, *pieces, *(state or ()))


def moved(value, axes, sizes, where):
    count, heads = sizes
    pairs = []
    for t in range(count):
        for h in range(heads):
            target = where(t, h)
            if target is not None:
                pairs.append((t * heads + h, target[0] * heads + target[1]))
    return lax.ppermute(value, axes, pairs)


def paired_body(queries, keys, values, lengths, out_weight):
    rows, width = queries.shape
    axes = ("tok", "head")
    sizes = count, heads = (lax.axis_size("tok"), lax.axis_size("head"))
    tok, head = lax.axis_index("tok"), lax.axis_index("head")
    side, level = tok % 2, tok // 2
    parity, core, half = level % 2, head % 2, head // 2
    send = functools.partial(moved, axes=axes, sizes=sizes)

    own = jnp.concatenate([keys, values], axis=1)
    back2 = send(own, where=lambda t, h: (t + 2, h) if t + 2 < count else None)
    weight_side = send(out_weight, where=lambda t, h: (t ^ 1, h))
    back4 = send(back2, where=lambda t, h: (t + 2, h) if t + 2 < count else None)
    back2_side = send(back2, where=lambda t, h: (t ^ 1, h))
    rest = jnp.where(side == 0, own, back4)
    rest = send(rest, where=lambda t, h: (t ^ 1, h))
    weight_far = send(out_weight, where=lambda t, h: (t ^ 4, h))
    weight_far_side = send(weight_far, where=lambda t, h: (t ^ 1, h))

    qpos = tok * rows + jnp.arange(rows, dtype=jnp.int32)
    start = doc_starts(lengths, qpos)[:, None]
    shift = lambda k: (tok - k) * rows
    near = jnp.stack([shift(0), shift(2), shift(2) + rows * (1 - 2 * side)])
    far = jnp.stack([shift(4), jnp.where(side == 0, shift(3), shift(1))])
    state = attend(queries, start, [own, back2, back2_side], near, True, None, False)
    attn = attend(queries, start, [back4, rest], far, False, state, True)
    attn_pair = send(attn, where=lambda t, h: (t ^ 2, h))

    mine = core == parity
    keep_rows = jnp.where(mine, attn, attn_pair)
    send_rows = jnp.where(mine, attn_pair, attn)

    def unit(weight, far_off):
        keeper = lambda t: (t // 4) ^ (1 if far_off else 0)
        keep = jnp.dot(keep_rows, weight, preferred_element_type=jnp.float32)
        away = jnp.dot(send_rows, weight, preferred_element_type=jnp.float32).astype(jnp.bfloat16)
        summed = keep + send(away, where=lambda t, h: (t, h ^ 1))
        low = summed.astype(jnp.bfloat16)
        got = send(low, where=lambda t, h: (t, h ^ 2) if (h // 2) != keeper(t) else None)
        total = (summed + got).astype(jnp.bfloat16)
        over = send(
            total,
            where=lambda t, h: (t ^ 2, h ^ 1)
            if (h // 2) == keeper(t) and (h % 2) != (t // 2) % 2
            else None,
        )
        return jnp.where(mine, total, over)

    near_same = unit(out_weight, False)
    near_side = unit(weight_side, False)
    far_same = unit(weight_far, True)
    far_side = unit(weight_far_side, True)
    is_near = half == level // 2
    same = jnp.where(is_near, near_same, far_same)
    other = jnp.where(is_near, near_side, far_side)
    return jnp.where(
        side == 0,
        jnp.concatenate([same, other], axis=1),
        jnp.concatenate([other, same], axis=1),
    )


def ring_body(queries, keys, values, lengths, out_weight):
    rows = queries.shape[0]
    count = lax.axis_size("tok")
    tok = lax.axis_index("tok")
    qpos = tok * rows + jnp.arange(rows, dtype=jnp.int32)
    start = doc_starts(lengths, qpos)[:, None]
    piece = jnp.concatenate([keys, values], axis=1)
    state = attend(queries, start, [piece], (tok * rows)[None], True, None, False)

    def advance(step, carried):
        piece, state = carried
        piece = lax.ppermute(piece, "tok", [(i, i + 1) for i in range(count - 1)])
        state = attend(queries, start, [piece], ((tok - step) * rows)[None], False, state, False)
        return piece, state

    piece, (acc, _) = lax.fori_loop(1, count // 2 + 1, advance, (piece, state))
    acc = acc.reshape(rows, -1, 2, HD)
    attn = (acc[:, :, 0] / acc[:, :, 1]).reshape(rows, -1).astype(jnp.bfloat16)
    terms = jnp.dot(
        attn,
        lax.all_gather(out_weight, "tok", axis=1, tiled=True),
        preferred_element_type=jnp.float32,
    )
    return lax.psum_scatter(terms.astype(jnp.bfloat16), "head", scatter_dimension=1, tiled=True)


def solution(mesh):
    count, heads = mesh.shape["tok"], mesh.shape["head"]
    body = paired_body if (count, heads) == (8, 4) else ring_body
    placed = (P("tok", "head"), P("tok", "head"), P("tok", "head"), P(), P("head", "tok"))
    return jax.shard_map(
        body, mesh=mesh, in_specs=placed, out_specs=P("tok", "head"), check_vma=False
    )
```

```python
import functools
import math

import jax
import jax.numpy as jnp
from jax import lax
from jax.experimental import pallas as pl
from jax.experimental.pallas import tpu as pltpu
from jax.sharding import PartitionSpec as P

QH = 32
KVH = 8
HD = 128
RATIO = QH // KVH
SCALE = 1.0 / HD**0.5
LOW = -1e30
STACK = 2


def doc_ends(lengths):
    order = jnp.arange(lengths.shape[0], dtype=jnp.int32)
    return jnp.sum(jnp.where(order[None, :] <= order[:, None], lengths[None, :], 0), axis=1)


def doc_starts(lengths, positions):
    ends = doc_ends(lengths)[None, :]
    return jnp.max(jnp.where(ends <= positions[:, None], ends, 0), axis=1)


def attend_kernel(count, own, resume, last, bases, q_ref, start_ref, *refs):
    pieces, refs = refs[:count], refs[count:]
    if resume:
        acc_in, top_in = refs[:2]
        refs = refs[2:]
    outs = refs[-1:] if last else refs[-2:]
    group = pl.program_id(0)
    groups = pieces[0].shape[1] // (2 * HD)
    rows = q_ref.shape[0]
    stack = STACK
    factor = SCALE * math.log2(math.e)
    start = jnp.concatenate([start_ref[...]] * stack, axis=0)

    def part(i, index):
        return pieces[i][:, pl.ds(pl.multiple_of(index * HD, HD), HD)]

    key = jnp.concatenate([part(i, group) for i in range(count)], axis=0)
    value = jnp.concatenate([part(i, groups + group) for i in range(count)], axis=0)
    value = jnp.concatenate([value, jnp.ones_like(value)], axis=1)

    def score(c):
        heads = range(c * stack, (c + 1) * stack)
        query = jnp.concatenate([q_ref[:, j * HD : (j + 1) * HD] for j in heads], axis=0)
        full = lax.dot_general(
            query, key, (((1,), (1,)), ((), ())), preferred_element_type=jnp.float32
        )
        scores = []
        at = 0
        for i in range(count):
            size = pieces[i].shape[0]
            s = full[:, at : at + size]
            at += size
            column = lax.broadcasted_iota(jnp.int32, s.shape, 1)
            allowed = column >= start - bases[i]
            if own and i == 0:
                row = lax.broadcasted_iota(jnp.int32, (rows, size), 0)
                allowed = allowed & (column <= jnp.concatenate([row] * stack, axis=0))
            scores.append(jnp.where(allowed, s, LOW))
        return scores

    def finish(c, scores):
        heads = range(c * stack, (c + 1) * stack)
        top = functools.reduce(jnp.maximum, [jnp.max(s, axis=1, keepdims=True) for s in scores])
        if resume:
            before = jnp.concatenate([top_in[:, j * HD : j * HD + 1] for j in heads], axis=0)
            top = jnp.maximum(top, before)
        weights = [jnp.exp2((s - top) * factor).astype(jnp.bfloat16) for s in scores]
        acc = jnp.dot(
            jnp.concatenate(weights, axis=1), value, preferred_element_type=jnp.float32
        )
        if resume:
            old = [acc_in[:, 2 * j * HD : 2 * (j + 1) * HD] for j in heads]
            acc = acc + jnp.concatenate(old, axis=0) * jnp.exp2((before - top) * factor)
        for n, j in enumerate(heads):
            mine = acc[n * rows : (n + 1) * rows]
            if last:
                ratio = mine[:, :HD] / mine[:, HD:]
                outs[0][:, j * HD : (j + 1) * HD] = ratio.astype(outs[0].dtype)
            else:
                outs[0][:, 2 * j * HD : 2 * (j + 1) * HD] = mine
                outs[1][:, j * HD : (j + 1) * HD] = jnp.broadcast_to(
                    top[n * rows : (n + 1) * rows], (rows, HD)
                )

    held = None
    for c in range(RATIO // stack):
        scores = score(c)
        if held is not None:
            finish(*held)
        held = (c, scores)
    finish(*held)


def attend(queries, start, pieces, bases, own, state, last, after=()):
    rows, width = queries.shape
    heads = width // HD
    groups = heads // RATIO
    count = len(pieces)
    resume = state is not None
    specs = [
        pl.BlockSpec((rows, RATIO * HD), lambda g, b: (0, g)),
        pl.BlockSpec((rows, 1), lambda g, b: (0, 0)),
    ]
    specs += [pl.BlockSpec(p.shape, lambda g, b: (0, 0)) for p in pieces]
    state_specs = [
        pl.BlockSpec((rows, 2 * RATIO * HD), lambda g, b: (0, g)),
        pl.BlockSpec((rows, RATIO * HD), lambda g, b: (0, g)),
    ]
    if resume:
        specs += state_specs
    specs += [pl.BlockSpec(memory_space=pl.ANY)] * len(after)
    if last:
        out_shape = jax.ShapeDtypeStruct((rows, width), jnp.bfloat16)
        out_specs = pl.BlockSpec((rows, RATIO * HD), lambda g, b: (0, g))
    else:
        out_shape = (
            jax.ShapeDtypeStruct((rows, 2 * width), jnp.float32),
            jax.ShapeDtypeStruct((rows, width), jnp.float32),
        )
        out_specs = tuple(state_specs)
    seen = sum(p.shape[0] for p in pieces)
    return pl.pallas_call(
        functools.partial(attend_kernel, count, own, resume, last),
        grid_spec=pltpu.PrefetchScalarGridSpec(
            num_scalar_prefetch=1,
            grid=(groups,),
            in_specs=specs,
            out_specs=out_specs,
        ),
        out_shape=out_shape,
        compiler_params=pltpu.CompilerParams(vmem_limit_bytes=40 * 2**20),
        cost_estimate=pl.CostEstimate(
            flops=6 * rows * seen * width,
            bytes_accessed=4 * rows * width,
            transcendentals=rows * seen * heads,
        ),
    )(bases, queries, start, *pieces, *(state or ()), *after)


def moved(value, axes, sizes, where):
    count, heads = sizes
    pairs = []
    for t in range(count):
        for h in range(heads):
            target = where(t, h)
            if target is not None:
                pairs.append((t * heads + h, target[0] * heads + target[1]))
    return lax.ppermute(value, axes, pairs)


def paired_body(queries, keys, values, lengths, out_weight):
    rows, width = queries.shape
    axes = ("tok", "head")
    sizes = count, heads = (lax.axis_size("tok"), lax.axis_size("head"))
    tok, head = lax.axis_index("tok"), lax.axis_index("head")
    side, level = tok % 2, tok // 2
    parity, core, half = level % 2, head % 2, head // 2
    send = functools.partial(moved, axes=axes, sizes=sizes)

    own = jnp.concatenate([keys, values], axis=1)
    back2 = send(own, where=lambda t, h: (t + 2, h) if t + 2 < count else None)
    weight_side = send(out_weight, where=lambda t, h: (t ^ 1, h))
    weight_down = send(out_weight, where=lambda t, h: (t - 4, h) if t >= 4 else None)
    back4 = send(back2, where=lambda t, h: (t + 2, h) if 2 <= t < count - 2 else None)
    back2_side = send(back2, where=lambda t, h: (t ^ 1, h) if t >= 2 else None)
    rest = jnp.where(side == 0, own, back4)
    rest = send(rest, where=lambda t, h: (t ^ 1, h) if t % 2 == 0 or t >= 4 else None)
    late, _ = lax.optimization_barrier((out_weight, back4))
    weight_up = send(late, where=lambda t, h: (t + 4, h) if t < 4 else None)
    weight_far = jnp.where(level < 2, weight_down, weight_up)
    weight_far_side = send(weight_far, where=lambda t, h: (t ^ 1, h))

    qpos = tok * rows + jnp.arange(rows, dtype=jnp.int32)
    start = doc_starts(lengths, qpos)[:, None]
    shift = lambda k: (tok - k) * rows
    first = jnp.stack([shift(0), shift(2)])
    second = jnp.stack([shift(2) + rows * (1 - 2 * side), shift(4)])
    third = jnp.where(side == 0, shift(3), shift(1))[None]
    state = attend(queries, start, [own, back2], first, True, None, False)
    state = attend(queries, start, [back2_side, back4], second, False, state, False)
    attn = attend(queries, start, [rest], third, False, state, True, (weight_side,))
    attn_pair = send(attn, where=lambda t, h: (t ^ 2, h))

    mine = core == parity
    keep_rows = jnp.where(mine, attn, attn_pair)
    send_rows = jnp.where(mine, attn_pair, attn)

    def unit(weight, far_off):
        keeper = lambda t: (t // 4) ^ (1 if far_off else 0)
        keep = jnp.dot(keep_rows, weight, preferred_element_type=jnp.float32)
        away = jnp.dot(send_rows, weight, preferred_element_type=jnp.float32).astype(jnp.bfloat16)
        summed = keep + send(away, where=lambda t, h: (t, h ^ 1))
        low = summed.astype(jnp.bfloat16)
        got = send(low, where=lambda t, h: (t, h ^ 2) if (h // 2) != keeper(t) else None)
        total = (summed + got).astype(jnp.bfloat16)
        over = send(
            total,
            where=lambda t, h: (t ^ 2, h ^ 1)
            if (h // 2) == keeper(t) and (h % 2) != (t // 2) % 2
            else None,
        )
        return jnp.where(mine, total, over)

    near_same = unit(out_weight, False)
    near_side = unit(weight_side, False)
    far_same = unit(weight_far, True)
    far_side = unit(weight_far_side, True)
    is_near = half == level // 2
    same = jnp.where(is_near, near_same, far_same)
    other = jnp.where(is_near, near_side, far_side)
    return jnp.where(
        side == 0,
        jnp.concatenate([same, other], axis=1),
        jnp.concatenate([other, same], axis=1),
    )


def ring_body(queries, keys, values, lengths, out_weight):
    rows = queries.shape[0]
    count = lax.axis_size("tok")
    tok = lax.axis_index("tok")
    qpos = tok * rows + jnp.arange(rows, dtype=jnp.int32)
    start = doc_starts(lengths, qpos)[:, None]
    piece = jnp.concatenate([keys, values], axis=1)
    state = attend(queries, start, [piece], (tok * rows)[None], True, None, False)

    def advance(step, carried):
        piece, state = carried
        piece = lax.ppermute(piece, "tok", [(i, i + 1) for i in range(count - 1)])
        state = attend(queries, start, [piece], ((tok - step) * rows)[None], False, state, False)
        return piece, state

    piece, (acc, _) = lax.fori_loop(1, count // 2 + 1, advance, (piece, state))
    acc = acc.reshape(rows, -1, 2, HD)
    attn = (acc[:, :, 0] / acc[:, :, 1]).reshape(rows, -1).astype(jnp.bfloat16)
    terms = jnp.dot(
        attn,
        lax.all_gather(out_weight, "tok", axis=1, tiled=True),
        preferred_element_type=jnp.float32,
    )
    return lax.psum_scatter(terms.astype(jnp.bfloat16), "head", scatter_dimension=1, tiled=True)


def solution(mesh):
    count, heads = mesh.shape["tok"], mesh.shape["head"]
    body = paired_body if (count, heads) == (8, 4) else ring_body
    placed = (P("tok", "head"), P("tok", "head"), P("tok", "head"), P(), P("head", "tok"))
    return jax.shard_map(
        body, mesh=mesh, in_specs=placed, out_specs=P("tok", "head"), check_vma=False
    )
```

```python
import functools
import math

import jax
import jax.numpy as jnp
from jax import lax
from jax.experimental import pallas as pl
from jax.experimental.pallas import tpu as pltpu
from jax.sharding import PartitionSpec as P

QH = 32
KVH = 8
HD = 128
RATIO = QH // KVH
SCALE = 1.0 / HD**0.5
LOW = -1e30
STACK = 2


def doc_ends(lengths):
    order = jnp.arange(lengths.shape[0], dtype=jnp.int32)
    return jnp.sum(jnp.where(order[None, :] <= order[:, None], lengths[None, :], 0), axis=1)


def doc_starts(lengths, positions):
    ends = doc_ends(lengths)[None, :]
    return jnp.max(jnp.where(ends <= positions[:, None], ends, 0), axis=1)


def attend_kernel(count, own, resume, last, bases, q_ref, start_ref, *refs):
    pieces, refs = refs[:count], refs[count:]
    if resume:
        acc_in, top_in = refs[:2]
        refs = refs[2:]
    outs = refs[-1:] if last else refs[-2:]
    group = pl.program_id(0)
    groups = pieces[0].shape[1] // (2 * HD)
    rows = q_ref.shape[0]
    stack = STACK
    factor = SCALE * math.log2(math.e)
    start = jnp.concatenate([start_ref[...]] * stack, axis=0)

    def part(i, index):
        return pieces[i][:, pl.ds(pl.multiple_of(index * HD, HD), HD)]

    key = jnp.concatenate([part(i, group) for i in range(count)], axis=0)
    value = jnp.concatenate([part(i, groups + group) for i in range(count)], axis=0)
    value = jnp.concatenate([value, jnp.ones_like(value)], axis=1)

    def score(c):
        heads = range(c * stack, (c + 1) * stack)
        query = jnp.concatenate([q_ref[:, j * HD : (j + 1) * HD] for j in heads], axis=0)
        full = lax.dot_general(
            query, key, (((1,), (1,)), ((), ())), preferred_element_type=jnp.float32
        )
        scores = []
        at = 0
        for i in range(count):
            size = pieces[i].shape[0]
            s = full[:, at : at + size]
            at += size
            column = lax.broadcasted_iota(jnp.int32, s.shape, 1)
            allowed = column >= start - bases[i]
            if own and i == 0:
                row = lax.broadcasted_iota(jnp.int32, (rows, size), 0)
                allowed = allowed & (column <= jnp.concatenate([row] * stack, axis=0))
            scores.append(jnp.where(allowed, s, LOW))
        return scores

    def finish(c, scores):
        heads = range(c * stack, (c + 1) * stack)
        top = functools.reduce(jnp.maximum, [jnp.max(s, axis=1, keepdims=True) for s in scores])
        if resume:
            before = jnp.concatenate([top_in[:, j * HD : j * HD + 1] for j in heads], axis=0)
            top = jnp.maximum(top, before)
        weights = [jnp.exp2((s - top) * factor).astype(jnp.bfloat16) for s in scores]
        acc = jnp.dot(
            jnp.concatenate(weights, axis=1), value, preferred_element_type=jnp.float32
        )
        if resume:
            old = [acc_in[:, 2 * j * HD : 2 * (j + 1) * HD] for j in heads]
            acc = acc + jnp.concatenate(old, axis=0) * jnp.exp2((before - top) * factor)
        for n, j in enumerate(heads):
            mine = acc[n * rows : (n + 1) * rows]
            if last:
                ratio = mine[:, :HD] / mine[:, HD:]
                outs[0][:, j * HD : (j + 1) * HD] = ratio.astype(outs[0].dtype)
            else:
                outs[0][:, 2 * j * HD : 2 * (j + 1) * HD] = mine
                outs[1][:, j * HD : (j + 1) * HD] = jnp.broadcast_to(
                    top[n * rows : (n + 1) * rows], (rows, HD)
                )

    held = None
    for c in range(RATIO // stack):
        scores = score(c)
        if held is not None:
            finish(*held)
        held = (c, scores)
    finish(*held)


def attend(queries, start, pieces, bases, own, state, last, after=()):
    rows, width = queries.shape
    heads = width // HD
    groups = heads // RATIO
    count = len(pieces)
    resume = state is not None
    specs = [
        pl.BlockSpec((rows, RATIO * HD), lambda g, b: (0, g)),
        pl.BlockSpec((rows, 1), lambda g, b: (0, 0)),
    ]
    specs += [pl.BlockSpec(p.shape, lambda g, b: (0, 0)) for p in pieces]
    state_specs = [
        pl.BlockSpec((rows, 2 * RATIO * HD), lambda g, b: (0, g)),
        pl.BlockSpec((rows, RATIO * HD), lambda g, b: (0, g)),
    ]
    if resume:
        specs += state_specs
    specs += [pl.BlockSpec(memory_space=pl.ANY)] * len(after)
    if last:
        out_shape = jax.ShapeDtypeStruct((rows, width), jnp.bfloat16)
        out_specs = pl.BlockSpec((rows, RATIO * HD), lambda g, b: (0, g))
    else:
        out_shape = (
            jax.ShapeDtypeStruct((rows, 2 * width), jnp.float32),
            jax.ShapeDtypeStruct((rows, width), jnp.float32),
        )
        out_specs = tuple(state_specs)
    seen = sum(p.shape[0] for p in pieces)
    return pl.pallas_call(
        functools.partial(attend_kernel, count, own, resume, last),
        grid_spec=pltpu.PrefetchScalarGridSpec(
            num_scalar_prefetch=1,
            grid=(groups,),
            in_specs=specs,
            out_specs=out_specs,
        ),
        out_shape=out_shape,
        compiler_params=pltpu.CompilerParams(vmem_limit_bytes=40 * 2**20),
        cost_estimate=pl.CostEstimate(
            flops=6 * rows * seen * width,
            bytes_accessed=4 * rows * width,
            transcendentals=rows * seen * heads,
        ),
    )(bases, queries, start, *pieces, *(state or ()), *after)


def moved(value, axes, sizes, where):
    count, heads = sizes
    pairs = []
    for t in range(count):
        for h in range(heads):
            target = where(t, h)
            if target is not None:
                pairs.append((t * heads + h, target[0] * heads + target[1]))
    return lax.ppermute(value, axes, pairs)


def beside_kernel(left, right, out):
    width = left.shape[1]
    out[:, :width] = left[...]
    out[:, width:] = right[...]


def beside(left, right):
    rows, width = left.shape
    return pl.pallas_call(
        beside_kernel, out_shape=jax.ShapeDtypeStruct((rows, 2 * width), left.dtype)
    )(left, right)


def paired_body(queries, keys, values, lengths, out_weight):
    rows, width = queries.shape
    axes = ("tok", "head")
    sizes = count, heads = (lax.axis_size("tok"), lax.axis_size("head"))
    tok, head = lax.axis_index("tok"), lax.axis_index("head")
    side, level = tok % 2, tok // 2
    parity, core, half = level % 2, head % 2, head // 2
    send = functools.partial(moved, axes=axes, sizes=sizes)

    own = beside(keys, values)
    back2 = send(own, where=lambda t, h: (t + 2, h) if t + 2 < count else None)
    weight_side = send(out_weight, where=lambda t, h: (t ^ 1, h))
    weight_down = send(out_weight, where=lambda t, h: (t - 4, h) if t >= 4 else None)
    back4 = send(back2, where=lambda t, h: (t + 2, h) if 2 <= t < count - 2 else None)
    back2_side = send(back2, where=lambda t, h: (t ^ 1, h) if t >= 2 else None)
    rest = jnp.where(side == 0, own, back4)
    rest = send(rest, where=lambda t, h: (t ^ 1, h) if t % 2 == 0 or t >= 4 else None)
    late, _ = lax.optimization_barrier((out_weight, back2))
    weight_up = send(late, where=lambda t, h: (t + 4, h) if t in (2, 3) else None)
    later, _ = lax.optimization_barrier((out_weight, back2_side))
    weight_up2 = send(later, where=lambda t, h: (t + 4, h) if t < 2 else None)
    weight_far = jnp.where(
        level < 2, weight_down, jnp.where(level == 2, weight_up2, weight_up)
    )
    weight_far_side = send(weight_far, where=lambda t, h: (t ^ 1, h))

    qpos = tok * rows + jnp.arange(rows, dtype=jnp.int32)
    start = doc_starts(lengths, qpos)[:, None]
    shift = lambda k: (tok - k) * rows
    first = jnp.stack([shift(0), shift(2)])
    second = jnp.stack([shift(2) + rows * (1 - 2 * side), shift(4)])
    third = jnp.where(side == 0, shift(3), shift(1))[None]
    state = attend(queries, start, [own, back2], first, True, None, False)
    state = attend(queries, start, [back2_side, back4], second, False, state, False)
    attn = attend(queries, start, [rest], third, False, state, True, (weight_side,))
    attn_pair = send(attn, where=lambda t, h: (t ^ 2, h))

    mine = core == parity
    keep_rows = jnp.where(mine, attn, attn_pair)
    send_rows = jnp.where(mine, attn_pair, attn)

    def unit(weight, far_off):
        keeper = lambda t: (t // 4) ^ (1 if far_off else 0)
        keep = jnp.dot(keep_rows, weight, preferred_element_type=jnp.float32)
        away = jnp.dot(send_rows, weight, preferred_element_type=jnp.float32).astype(jnp.bfloat16)
        summed = keep + send(away, where=lambda t, h: (t, h ^ 1))
        low = summed.astype(jnp.bfloat16)
        got = send(low, where=lambda t, h: (t, h ^ 2) if (h // 2) != keeper(t) else None)
        total = (summed + got).astype(jnp.bfloat16)
        over = send(
            total,
            where=lambda t, h: (t ^ 2, h ^ 1)
            if (h // 2) == keeper(t) and (h % 2) != (t // 2) % 2
            else None,
        )
        return jnp.where(mine, total, over)

    near_same = unit(out_weight, False)
    near_side = unit(weight_side, False)
    far_same = unit(weight_far, True)
    far_side = unit(weight_far_side, True)
    is_near = half == level // 2
    same = jnp.where(is_near, near_same, far_same)
    other = jnp.where(is_near, near_side, far_side)
    return jnp.where(
        side == 0,
        jnp.concatenate([same, other], axis=1),
        jnp.concatenate([other, same], axis=1),
    )


def ring_body(queries, keys, values, lengths, out_weight):
    rows = queries.shape[0]
    count = lax.axis_size("tok")
    tok = lax.axis_index("tok")
    qpos = tok * rows + jnp.arange(rows, dtype=jnp.int32)
    start = doc_starts(lengths, qpos)[:, None]
    piece = jnp.concatenate([keys, values], axis=1)
    state = attend(queries, start, [piece], (tok * rows)[None], True, None, False)

    def advance(step, carried):
        piece, state = carried
        piece = lax.ppermute(piece, "tok", [(i, i + 1) for i in range(count - 1)])
        state = attend(queries, start, [piece], ((tok - step) * rows)[None], False, state, False)
        return piece, state

    piece, (acc, _) = lax.fori_loop(1, count // 2 + 1, advance, (piece, state))
    acc = acc.reshape(rows, -1, 2, HD)
    attn = (acc[:, :, 0] / acc[:, :, 1]).reshape(rows, -1).astype(jnp.bfloat16)
    terms = jnp.dot(
        attn,
        lax.all_gather(out_weight, "tok", axis=1, tiled=True),
        preferred_element_type=jnp.float32,
    )
    return lax.psum_scatter(terms.astype(jnp.bfloat16), "head", scatter_dimension=1, tiled=True)


def solution(mesh):
    count, heads = mesh.shape["tok"], mesh.shape["head"]
    body = paired_body if (count, heads) == (8, 4) else ring_body
    placed = (P("tok", "head"), P("tok", "head"), P("tok", "head"), P(), P("head", "tok"))
    return jax.shard_map(
        body, mesh=mesh, in_specs=placed, out_specs=P("tok", "head"), check_vma=False
    )
```

```python
import functools
import math

import jax
import jax.numpy as jnp
from jax import lax
from jax.experimental import pallas as pl
from jax.experimental.pallas import tpu as pltpu
from jax.sharding import PartitionSpec as P

QH = 32
KVH = 8
HD = 128
RATIO = QH // KVH
SCALE = 1.0 / HD**0.5
LOW = -1e30
STACK = 2


def doc_ends(lengths):
    order = jnp.arange(lengths.shape[0], dtype=jnp.int32)
    return jnp.sum(jnp.where(order[None, :] <= order[:, None], lengths[None, :], 0), axis=1)


def doc_starts(lengths, positions):
    ends = doc_ends(lengths)[None, :]
    return jnp.max(jnp.where(ends <= positions[:, None], ends, 0), axis=1)


def attend_kernel(count, own, resume, last, bases, q_ref, start_ref, *refs):
    pieces, refs = refs[:count], refs[count:]
    if resume:
        acc_in, top_in = refs[:2]
        refs = refs[2:]
    outs = refs[-1:] if last else refs[-2:]
    group = pl.program_id(0)
    groups = pieces[0].shape[1] // (2 * HD)
    rows = q_ref.shape[0]
    stack = STACK
    factor = SCALE * math.log2(math.e)
    start = jnp.concatenate([start_ref[...]] * stack, axis=0)

    def part(i, index):
        return pieces[i][:, pl.ds(pl.multiple_of(index * HD, HD), HD)]

    key = jnp.concatenate([part(i, group) for i in range(count)], axis=0)
    value = jnp.concatenate([part(i, groups + group) for i in range(count)], axis=0)
    value = jnp.concatenate([value, jnp.ones_like(value)], axis=1)

    def score(c):
        heads = range(c * stack, (c + 1) * stack)
        query = jnp.concatenate([q_ref[:, j * HD : (j + 1) * HD] for j in heads], axis=0)
        full = lax.dot_general(
            query, key, (((1,), (1,)), ((), ())), preferred_element_type=jnp.float32
        )
        scores = []
        at = 0
        for i in range(count):
            size = pieces[i].shape[0]
            s = full[:, at : at + size]
            at += size
            column = lax.broadcasted_iota(jnp.int32, s.shape, 1)
            allowed = column >= start - bases[i]
            if own and i == 0:
                row = lax.broadcasted_iota(jnp.int32, (rows, size), 0)
                allowed = allowed & (column <= jnp.concatenate([row] * stack, axis=0))
            scores.append(jnp.where(allowed, s, LOW))
        return scores

    def finish(c, scores):
        heads = range(c * stack, (c + 1) * stack)
        top = functools.reduce(jnp.maximum, [jnp.max(s, axis=1, keepdims=True) for s in scores])
        if resume:
            before = jnp.concatenate([top_in[:, j * HD : j * HD + 1] for j in heads], axis=0)
            top = jnp.maximum(top, before)
        weights = [jnp.exp2((s - top) * factor).astype(jnp.bfloat16) for s in scores]
        acc = jnp.dot(
            jnp.concatenate(weights, axis=1), value, preferred_element_type=jnp.float32
        )
        if resume:
            old = [acc_in[:, 2 * j * HD : 2 * (j + 1) * HD] for j in heads]
            acc = acc + jnp.concatenate(old, axis=0) * jnp.exp2((before - top) * factor)
        for n, j in enumerate(heads):
            mine = acc[n * rows : (n + 1) * rows]
            if last:
                ratio = mine[:, :HD] / mine[:, HD:]
                outs[0][:, j * HD : (j + 1) * HD] = ratio.astype(outs[0].dtype)
            else:
                outs[0][:, 2 * j * HD : 2 * (j + 1) * HD] = mine
                outs[1][:, j * HD : (j + 1) * HD] = jnp.broadcast_to(
                    top[n * rows : (n + 1) * rows], (rows, HD)
                )

    held = None
    for c in range(RATIO // stack):
        scores = score(c)
        if held is not None:
            finish(*held)
        held = (c, scores)
    finish(*held)


def attend(queries, start, pieces, bases, own, state, last, after=()):
    rows, width = queries.shape
    heads = width // HD
    groups = heads // RATIO
    count = len(pieces)
    resume = state is not None
    specs = [
        pl.BlockSpec((rows, RATIO * HD), lambda g, b: (0, g)),
        pl.BlockSpec((rows, 1), lambda g, b: (0, 0)),
    ]
    specs += [pl.BlockSpec(p.shape, lambda g, b: (0, 0)) for p in pieces]
    state_specs = [
        pl.BlockSpec((rows, 2 * RATIO * HD), lambda g, b: (0, g)),
        pl.BlockSpec((rows, RATIO * HD), lambda g, b: (0, g)),
    ]
    if resume:
        specs += state_specs
    specs += [pl.BlockSpec(memory_space=pl.ANY)] * len(after)
    if last:
        out_shape = jax.ShapeDtypeStruct((rows, width), jnp.bfloat16)
        out_specs = pl.BlockSpec((rows, RATIO * HD), lambda g, b: (0, g))
    else:
        out_shape = (
            jax.ShapeDtypeStruct((rows, 2 * width), jnp.float32),
            jax.ShapeDtypeStruct((rows, width), jnp.float32),
        )
        out_specs = tuple(state_specs)
    seen = sum(p.shape[0] for p in pieces)
    return pl.pallas_call(
        functools.partial(attend_kernel, count, own, resume, last),
        grid_spec=pltpu.PrefetchScalarGridSpec(
            num_scalar_prefetch=1,
            grid=(groups,),
            in_specs=specs,
            out_specs=out_specs,
        ),
        out_shape=out_shape,
        compiler_params=pltpu.CompilerParams(vmem_limit_bytes=40 * 2**20),
        cost_estimate=pl.CostEstimate(
            flops=6 * rows * seen * width,
            bytes_accessed=4 * rows * width,
            transcendentals=rows * seen * heads,
        ),
    )(bases, queries, start, *pieces, *(state or ()), *after)


def moved(value, axes, sizes, where):
    count, heads = sizes
    pairs = []
    for t in range(count):
        for h in range(heads):
            target = where(t, h)
            if target is not None:
                pairs.append((t * heads + h, target[0] * heads + target[1]))
    return lax.ppermute(value, axes, pairs)


def beside_kernel(left, right, out):
    width = left.shape[1]
    out[:, :width] = left[...]
    out[:, width:] = right[...]


def beside(left, right):
    rows, width = left.shape
    return pl.pallas_call(
        beside_kernel, out_shape=jax.ShapeDtypeStruct((rows, 2 * width), left.dtype)
    )(left, right)


def paired_body(queries, keys, values, lengths, out_weight):
    rows, width = queries.shape
    axes = ("tok", "head")
    sizes = count, heads = (lax.axis_size("tok"), lax.axis_size("head"))
    tok, head = lax.axis_index("tok"), lax.axis_index("head")
    side, level = tok % 2, tok // 2
    parity, core, half = level % 2, head % 2, head // 2
    send = functools.partial(moved, axes=axes, sizes=sizes)

    own = beside(keys, values)
    back2 = send(own, where=lambda t, h: (t + 2, h) if t + 2 < count else None)
    weight_side = send(out_weight, where=lambda t, h: (t ^ 1, h))
    weight_down = send(out_weight, where=lambda t, h: (t - 4, h) if t >= 4 else None)
    back4 = send(back2, where=lambda t, h: (t + 2, h) if 2 <= t < count - 2 else None)
    back2_side = send(back2, where=lambda t, h: (t ^ 1, h) if t >= 2 else None)
    rest = jnp.where(side == 0, own, back4)
    rest = send(rest, where=lambda t, h: (t ^ 1, h) if t % 2 == 0 or t >= 4 else None)
    late, _ = lax.optimization_barrier((out_weight, back2))
    weight_up = send(late, where=lambda t, h: (t + 4, h) if t in (2, 3) else None)
    later, _ = lax.optimization_barrier((out_weight, back2_side))
    weight_up2 = send(later, where=lambda t, h: (t + 4, h) if t < 2 else None)
    wide = out_weight.shape[1] // 2
    weight_far, weight_far_side = [], []
    for c in (slice(0, wide), slice(wide, None)):
        part = jnp.where(
            level < 2, weight_down[:, c], jnp.where(level == 2, weight_up2[:, c], weight_up[:, c])
        )
        weight_far.append(part)
        weight_far_side.append(send(part, where=lambda t, h: (t ^ 1, h)))

    qpos = tok * rows + jnp.arange(rows, dtype=jnp.int32)
    start = doc_starts(lengths, qpos)[:, None]
    shift = lambda k: (tok - k) * rows
    first = jnp.stack([shift(0), shift(2)])
    second = jnp.stack([shift(2) + rows * (1 - 2 * side), shift(4)])
    third = jnp.where(side == 0, shift(3), shift(1))[None]
    state = attend(queries, start, [own, back2], first, True, None, False)
    state = attend(queries, start, [back2_side, back4], second, False, state, False)
    attn = attend(queries, start, [rest], third, False, state, True, (weight_side,))
    attn_pair = send(attn, where=lambda t, h: (t ^ 2, h))

    mine = core == parity
    keep_rows = jnp.where(mine, attn, attn_pair)
    send_rows = jnp.where(mine, attn_pair, attn)

    def unit(weight, far_off):
        keeper = lambda t: (t // 4) ^ (1 if far_off else 0)
        def product(lines):
            parts = [jnp.dot(lines, w, preferred_element_type=jnp.float32) for w in weight]
            return parts[0] if len(parts) == 1 else jnp.concatenate(parts, axis=1)

        keep = product(keep_rows)
        away = product(send_rows).astype(jnp.bfloat16)
        summed = keep + send(away, where=lambda t, h: (t, h ^ 1))
        low = summed.astype(jnp.bfloat16)
        got = send(low, where=lambda t, h: (t, h ^ 2) if (h // 2) != keeper(t) else None)
        total = (summed + got).astype(jnp.bfloat16)
        over = send(
            total,
            where=lambda t, h: (t ^ 2, h ^ 1)
            if (h // 2) == keeper(t) and (h % 2) != (t // 2) % 2
            else None,
        )
        return jnp.where(mine, total, over)

    near_same = unit([out_weight], False)
    near_side = unit([weight_side], False)
    far_same = unit(weight_far, True)
    far_side = [unit([w], True) for w in weight_far_side]
    far_side = jnp.concatenate(far_side, axis=1)
    is_near = half == level // 2
    same = jnp.where(is_near, near_same, far_same)
    other = jnp.where(is_near, near_side, far_side)
    return jnp.where(
        side == 0,
        jnp.concatenate([same, other], axis=1),
        jnp.concatenate([other, same], axis=1),
    )


def ring_body(queries, keys, values, lengths, out_weight):
    rows = queries.shape[0]
    count = lax.axis_size("tok")
    tok = lax.axis_index("tok")
    qpos = tok * rows + jnp.arange(rows, dtype=jnp.int32)
    start = doc_starts(lengths, qpos)[:, None]
    piece = jnp.concatenate([keys, values], axis=1)
    state = attend(queries, start, [piece], (tok * rows)[None], True, None, False)

    def advance(step, carried):
        piece, state = carried
        piece = lax.ppermute(piece, "tok", [(i, i + 1) for i in range(count - 1)])
        state = attend(queries, start, [piece], ((tok - step) * rows)[None], False, state, False)
        return piece, state

    piece, (acc, _) = lax.fori_loop(1, count // 2 + 1, advance, (piece, state))
    acc = acc.reshape(rows, -1, 2, HD)
    attn = (acc[:, :, 0] / acc[:, :, 1]).reshape(rows, -1).astype(jnp.bfloat16)
    terms = jnp.dot(
        attn,
        lax.all_gather(out_weight, "tok", axis=1, tiled=True),
        preferred_element_type=jnp.float32,
    )
    return lax.psum_scatter(terms.astype(jnp.bfloat16), "head", scatter_dimension=1, tiled=True)


def solution(mesh):
    count, heads = mesh.shape["tok"], mesh.shape["head"]
    body = paired_body if (count, heads) == (8, 4) else ring_body
    placed = (P("tok", "head"), P("tok", "head"), P("tok", "head"), P(), P("head", "tok"))
    return jax.shard_map(
        body, mesh=mesh, in_specs=placed, out_specs=P("tok", "head"), check_vma=False
    )
```

```python
import functools
import math

import jax
import jax.numpy as jnp
from jax import lax
from jax.experimental import pallas as pl
from jax.experimental.pallas import tpu as pltpu
from jax.sharding import PartitionSpec as P

QH = 32
KVH = 8
HD = 128
RATIO = QH // KVH
SCALE = 1.0 / HD**0.5
LOW = -1e30
STACK = 2


def doc_ends(lengths):
    order = jnp.arange(lengths.shape[0], dtype=jnp.int32)
    return jnp.sum(jnp.where(order[None, :] <= order[:, None], lengths[None, :], 0), axis=1)


def doc_starts(lengths, positions):
    ends = doc_ends(lengths)[None, :]
    return jnp.max(jnp.where(ends <= positions[:, None], ends, 0), axis=1)


def attend_kernel(count, own, resume, last, bases, q_ref, start_ref, *refs):
    pieces, refs = refs[:count], refs[count:]
    if resume:
        acc_in, top_in = refs[:2]
        refs = refs[2:]
    outs = refs[-1:] if last else refs[-2:]
    group = pl.program_id(0)
    groups = pieces[0].shape[1] // (2 * HD)
    rows = q_ref.shape[0]
    stack = STACK
    factor = SCALE * math.log2(math.e)
    start = jnp.concatenate([start_ref[...]] * stack, axis=0)

    def part(i, index):
        return pieces[i][:, pl.ds(pl.multiple_of(index * HD, HD), HD)]

    key = jnp.concatenate([part(i, group) for i in range(count)], axis=0)
    value = jnp.concatenate([part(i, groups + group) for i in range(count)], axis=0)
    value = jnp.concatenate([value, jnp.ones_like(value)], axis=1)

    def score(c):
        heads = range(c * stack, (c + 1) * stack)
        query = jnp.concatenate([q_ref[:, j * HD : (j + 1) * HD] for j in heads], axis=0)
        full = lax.dot_general(
            query, key, (((1,), (1,)), ((), ())), preferred_element_type=jnp.float32
        )
        scores = []
        at = 0
        for i in range(count):
            size = pieces[i].shape[0]
            s = full[:, at : at + size]
            at += size
            column = lax.broadcasted_iota(jnp.int32, s.shape, 1)
            allowed = column >= start - bases[i]
            if own and i == 0:
                row = lax.broadcasted_iota(jnp.int32, (rows, size), 0)
                allowed = allowed & (column <= jnp.concatenate([row] * stack, axis=0))
            scores.append(jnp.where(allowed, s, LOW))
        return scores

    def finish(c, scores):
        heads = range(c * stack, (c + 1) * stack)
        top = functools.reduce(jnp.maximum, [jnp.max(s, axis=1, keepdims=True) for s in scores])
        if resume:
            before = jnp.concatenate([top_in[:, j * HD : j * HD + 1] for j in heads], axis=0)
            top = jnp.maximum(top, before)
        weights = [jnp.exp2((s - top) * factor).astype(jnp.bfloat16) for s in scores]
        acc = jnp.dot(
            jnp.concatenate(weights, axis=1), value, preferred_element_type=jnp.float32
        )
        if resume:
            old = [acc_in[:, 2 * j * HD : 2 * (j + 1) * HD] for j in heads]
            acc = acc + jnp.concatenate(old, axis=0) * jnp.exp2((before - top) * factor)
        for n, j in enumerate(heads):
            mine = acc[n * rows : (n + 1) * rows]
            if last:
                ratio = mine[:, :HD] / mine[:, HD:]
                outs[0][:, j * HD : (j + 1) * HD] = ratio.astype(outs[0].dtype)
            else:
                outs[0][:, 2 * j * HD : 2 * (j + 1) * HD] = mine
                outs[1][:, j * HD : (j + 1) * HD] = jnp.broadcast_to(
                    top[n * rows : (n + 1) * rows], (rows, HD)
                )

    held = None
    for c in range(RATIO // stack):
        scores = score(c)
        if held is not None:
            finish(*held)
        held = (c, scores)
    finish(*held)


def attend(queries, start, pieces, bases, own, state, last, after=()):
    rows, width = queries.shape
    heads = width // HD
    groups = heads // RATIO
    count = len(pieces)
    resume = state is not None
    specs = [
        pl.BlockSpec((rows, RATIO * HD), lambda g, b: (0, g)),
        pl.BlockSpec((rows, 1), lambda g, b: (0, 0)),
    ]
    specs += [pl.BlockSpec(p.shape, lambda g, b: (0, 0)) for p in pieces]
    state_specs = [
        pl.BlockSpec((rows, 2 * RATIO * HD), lambda g, b: (0, g)),
        pl.BlockSpec((rows, RATIO * HD), lambda g, b: (0, g)),
    ]
    if resume:
        specs += state_specs
    specs += [pl.BlockSpec(memory_space=pl.ANY)] * len(after)
    if last:
        out_shape = jax.ShapeDtypeStruct((rows, width), jnp.bfloat16)
        out_specs = pl.BlockSpec((rows, RATIO * HD), lambda g, b: (0, g))
    else:
        out_shape = (
            jax.ShapeDtypeStruct((rows, 2 * width), jnp.float32),
            jax.ShapeDtypeStruct((rows, width), jnp.float32),
        )
        out_specs = tuple(state_specs)
    seen = sum(p.shape[0] for p in pieces)
    return pl.pallas_call(
        functools.partial(attend_kernel, count, own, resume, last),
        grid_spec=pltpu.PrefetchScalarGridSpec(
            num_scalar_prefetch=1,
            grid=(groups,),
            in_specs=specs,
            out_specs=out_specs,
        ),
        out_shape=out_shape,
        compiler_params=pltpu.CompilerParams(vmem_limit_bytes=40 * 2**20),
        cost_estimate=pl.CostEstimate(
            flops=12 * rows * seen * width,
            bytes_accessed=4 * rows * width,
            transcendentals=rows * seen * heads,
        ),
    )(bases, queries, start, *pieces, *(state or ()), *after)


def moved(value, axes, sizes, where):
    count, heads = sizes
    pairs = []
    for t in range(count):
        for h in range(heads):
            target = where(t, h)
            if target is not None:
                pairs.append((t * heads + h, target[0] * heads + target[1]))
    return lax.ppermute(value, axes, pairs)


def beside_kernel(left, right, out):
    width = left.shape[1]
    out[:, :width] = left[...]
    out[:, width:] = right[...]


def beside(left, right):
    rows, width = left.shape
    return pl.pallas_call(
        beside_kernel, out_shape=jax.ShapeDtypeStruct((rows, 2 * width), left.dtype)
    )(left, right)


def paired_body(queries, keys, values, lengths, out_weight):
    rows, width = queries.shape
    axes = ("tok", "head")
    sizes = count, heads = (lax.axis_size("tok"), lax.axis_size("head"))
    tok, head = lax.axis_index("tok"), lax.axis_index("head")
    side, level = tok % 2, tok // 2
    parity, core, half = level % 2, head % 2, head // 2
    send = functools.partial(moved, axes=axes, sizes=sizes)

    own = beside(keys, values)
    back2 = send(own, where=lambda t, h: (t + 2, h) if t + 2 < count else None)
    weight_side = send(out_weight, where=lambda t, h: (t ^ 1, h))
    weight_down = send(out_weight, where=lambda t, h: (t - 4, h) if t >= 4 else None)
    back4 = send(back2, where=lambda t, h: (t + 2, h) if 2 <= t < count - 2 else None)
    back2_side = send(back2, where=lambda t, h: (t ^ 1, h) if t >= 2 else None)
    rest = jnp.where(side == 0, own, back4)
    rest = send(rest, where=lambda t, h: (t ^ 1, h) if t % 2 == 0 or t >= 4 else None)
    late, _ = lax.optimization_barrier((out_weight, back2))
    weight_up = send(late, where=lambda t, h: (t + 4, h) if t in (2, 3) else None)
    later, _ = lax.optimization_barrier((out_weight, back2_side))
    weight_up2 = send(later, where=lambda t, h: (t + 4, h) if t < 2 else None)
    wide = out_weight.shape[1] // 2
    weight_far, weight_far_side = [], []
    for c in (slice(0, wide), slice(wide, None)):
        part = jnp.where(
            level < 2, weight_down[:, c], jnp.where(level == 2, weight_up2[:, c], weight_up[:, c])
        )
        weight_far.append(part)
        weight_far_side.append(send(part, where=lambda t, h: (t ^ 1, h)))

    qpos = tok * rows + jnp.arange(rows, dtype=jnp.int32)
    start = doc_starts(lengths, qpos)[:, None]
    shift = lambda k: (tok - k) * rows
    first = jnp.stack([shift(0), shift(2)])
    second = jnp.stack([shift(2) + rows * (1 - 2 * side), shift(4)])
    third = jnp.where(side == 0, shift(3), shift(1))[None]
    state = attend(queries, start, [own, back2], first, True, None, False)
    state = attend(queries, start, [back2_side, back4], second, False, state, False)
    attn = attend(queries, start, [rest], third, False, state, True, (weight_side,))
    attn_pair = send(attn, where=lambda t, h: (t ^ 2, h))

    mine = core == parity
    keep_rows = jnp.where(mine, attn, attn_pair)
    send_rows = jnp.where(mine, attn_pair, attn)

    def unit(weight, far_off):
        keeper = lambda t: (t // 4) ^ (1 if far_off else 0)
        def product(lines):
            parts = [jnp.dot(lines, w, preferred_element_type=jnp.float32) for w in weight]
            return parts[0] if len(parts) == 1 else jnp.concatenate(parts, axis=1)

        keep = product(keep_rows)
        away = product(send_rows).astype(jnp.bfloat16)
        summed = keep + send(away, where=lambda t, h: (t, h ^ 1))
        low = summed.astype(jnp.bfloat16)
        got = send(low, where=lambda t, h: (t, h ^ 2) if (h // 2) != keeper(t) else None)
        total = (summed + got).astype(jnp.bfloat16)
        over = send(
            total,
            where=lambda t, h: (t ^ 2, h ^ 1)
            if (h // 2) == keeper(t) and (h % 2) != (t // 2) % 2
            else None,
        )
        return jnp.where(mine, total, over)

    near_same = unit([out_weight], False)
    near_side = unit([weight_side], False)
    far_same = unit(weight_far, True)
    far_side = [unit([w], True) for w in weight_far_side]
    far_side = jnp.concatenate(far_side, axis=1)
    is_near = half == level // 2
    same = jnp.where(is_near, near_same, far_same)
    other = jnp.where(is_near, near_side, far_side)
    return jnp.where(
        side == 0,
        jnp.concatenate([same, other], axis=1),
        jnp.concatenate([other, same], axis=1),
    )


def ring_body(queries, keys, values, lengths, out_weight):
    rows = queries.shape[0]
    count = lax.axis_size("tok")
    tok = lax.axis_index("tok")
    qpos = tok * rows + jnp.arange(rows, dtype=jnp.int32)
    start = doc_starts(lengths, qpos)[:, None]
    piece = jnp.concatenate([keys, values], axis=1)
    state = attend(queries, start, [piece], (tok * rows)[None], True, None, False)

    def advance(step, carried):
        piece, state = carried
        piece = lax.ppermute(piece, "tok", [(i, i + 1) for i in range(count - 1)])
        state = attend(queries, start, [piece], ((tok - step) * rows)[None], False, state, False)
        return piece, state

    piece, (acc, _) = lax.fori_loop(1, count // 2 + 1, advance, (piece, state))
    acc = acc.reshape(rows, -1, 2, HD)
    attn = (acc[:, :, 0] / acc[:, :, 1]).reshape(rows, -1).astype(jnp.bfloat16)
    terms = jnp.dot(
        attn,
        lax.all_gather(out_weight, "tok", axis=1, tiled=True),
        preferred_element_type=jnp.float32,
    )
    return lax.psum_scatter(terms.astype(jnp.bfloat16), "head", scatter_dimension=1, tiled=True)


def solution(mesh):
    count, heads = mesh.shape["tok"], mesh.shape["head"]
    body = paired_body if (count, heads) == (8, 4) else ring_body
    placed = (P("tok", "head"), P("tok", "head"), P("tok", "head"), P(), P("head", "tok"))
    return jax.shard_map(
        body, mesh=mesh, in_specs=placed, out_specs=P("tok", "head"), check_vma=False
    )
```

```python
import functools
import math

import jax
import jax.numpy as jnp
from jax import lax
from jax.experimental import pallas as pl
from jax.experimental.pallas import tpu as pltpu
from jax.sharding import PartitionSpec as P

QH = 32
KVH = 8
HD = 128
RATIO = QH // KVH
SCALE = 1.0 / HD**0.5
LOW = -1e30
STACK = 1


def doc_ends(lengths):
    order = jnp.arange(lengths.shape[0], dtype=jnp.int32)
    return jnp.sum(jnp.where(order[None, :] <= order[:, None], lengths[None, :], 0), axis=1)


def doc_starts(lengths, positions):
    ends = doc_ends(lengths)[None, :]
    return jnp.max(jnp.where(ends <= positions[:, None], ends, 0), axis=1)


def attend_kernel(count, own, resume, last, bases, q_ref, start_ref, *refs):
    pieces, refs = refs[:count], refs[count:]
    if resume:
        acc_in, top_in = refs[:2]
        refs = refs[2:]
    outs = refs[-1:] if last else refs[-2:]
    group = pl.program_id(0)
    groups = pieces[0].shape[1] // (2 * HD)
    rows = q_ref.shape[0]
    stack = STACK
    factor = SCALE * math.log2(math.e)
    start = jnp.concatenate([start_ref[...]] * stack, axis=0)

    def part(i, index):
        return pieces[i][:, pl.ds(pl.multiple_of(index * HD, HD), HD)]

    key = jnp.concatenate([part(i, group) for i in range(count)], axis=0)
    value = jnp.concatenate([part(i, groups + group) for i in range(count)], axis=0)
    value = jnp.concatenate([value, jnp.ones_like(value)], axis=1)

    def score(c):
        heads = range(c * stack, (c + 1) * stack)
        query = jnp.concatenate([q_ref[:, j * HD : (j + 1) * HD] for j in heads], axis=0)
        full = lax.dot_general(
            query, key, (((1,), (1,)), ((), ())), preferred_element_type=jnp.float32
        )
        scores = []
        at = 0
        for i in range(count):
            size = pieces[i].shape[0]
            s = full[:, at : at + size]
            at += size
            column = lax.broadcasted_iota(jnp.int32, s.shape, 1)
            allowed = column >= start - bases[i]
            if own and i == 0:
                row = lax.broadcasted_iota(jnp.int32, (rows, size), 0)
                allowed = allowed & (column <= jnp.concatenate([row] * stack, axis=0))
            scores.append(jnp.where(allowed, s, LOW))
        return scores

    def finish(c, scores):
        heads = range(c * stack, (c + 1) * stack)
        top = functools.reduce(jnp.maximum, [jnp.max(s, axis=1, keepdims=True) for s in scores])
        if resume:
            before = jnp.concatenate([top_in[:, j * HD : j * HD + 1] for j in heads], axis=0)
            top = jnp.maximum(top, before)
        weights = [jnp.exp2((s - top) * factor).astype(jnp.bfloat16) for s in scores]
        acc = jnp.dot(
            jnp.concatenate(weights, axis=1), value, preferred_element_type=jnp.float32
        )
        if resume:
            old = [acc_in[:, 2 * j * HD : 2 * (j + 1) * HD] for j in heads]
            acc = acc + jnp.concatenate(old, axis=0) * jnp.exp2((before - top) * factor)
        for n, j in enumerate(heads):
            mine = acc[n * rows : (n + 1) * rows]
            if last:
                ratio = mine[:, :HD] / mine[:, HD:]
                outs[0][:, j * HD : (j + 1) * HD] = ratio.astype(outs[0].dtype)
            else:
                outs[0][:, 2 * j * HD : 2 * (j + 1) * HD] = mine
                outs[1][:, j * HD : (j + 1) * HD] = jnp.broadcast_to(
                    top[n * rows : (n + 1) * rows], (rows, HD)
                )

    held = None
    for c in range(RATIO // stack):
        scores = score(c)
        if held is not None:
            finish(*held)
        held = (c, scores)
    finish(*held)


def attend(queries, start, pieces, bases, own, state, last, after=()):
    rows, width = queries.shape
    heads = width // HD
    groups = heads // RATIO
    count = len(pieces)
    resume = state is not None
    specs = [
        pl.BlockSpec((rows, RATIO * HD), lambda g, b: (0, g)),
        pl.BlockSpec((rows, 1), lambda g, b: (0, 0)),
    ]
    specs += [pl.BlockSpec(p.shape, lambda g, b: (0, 0)) for p in pieces]
    state_specs = [
        pl.BlockSpec((rows, 2 * RATIO * HD), lambda g, b: (0, g)),
        pl.BlockSpec((rows, RATIO * HD), lambda g, b: (0, g)),
    ]
    if resume:
        specs += state_specs
    specs += [pl.BlockSpec(memory_space=pl.ANY)] * len(after)
    if last:
        out_shape = jax.ShapeDtypeStruct((rows, width), jnp.bfloat16)
        out_specs = pl.BlockSpec((rows, RATIO * HD), lambda g, b: (0, g))
    else:
        out_shape = (
            jax.ShapeDtypeStruct((rows, 2 * width), jnp.float32),
            jax.ShapeDtypeStruct((rows, width), jnp.float32),
        )
        out_specs = tuple(state_specs)
    seen = sum(p.shape[0] for p in pieces)
    return pl.pallas_call(
        functools.partial(attend_kernel, count, own, resume, last),
        grid_spec=pltpu.PrefetchScalarGridSpec(
            num_scalar_prefetch=1,
            grid=(groups,),
            in_specs=specs,
            out_specs=out_specs,
        ),
        out_shape=out_shape,
        compiler_params=pltpu.CompilerParams(vmem_limit_bytes=40 * 2**20),
        cost_estimate=pl.CostEstimate(
            flops=12 * rows * seen * width,
            bytes_accessed=4 * rows * width,
            transcendentals=rows * seen * heads,
        ),
    )(bases, queries, start, *pieces, *(state or ()), *after)


def moved(value, axes, sizes, where):
    count, heads = sizes
    pairs = []
    for t in range(count):
        for h in range(heads):
            target = where(t, h)
            if target is not None:
                pairs.append((t * heads + h, target[0] * heads + target[1]))
    return lax.ppermute(value, axes, pairs)


def beside_kernel(left, right, out):
    width = left.shape[1]
    out[:, :width] = left[...]
    out[:, width:] = right[...]


def beside(left, right):
    rows, width = left.shape
    return pl.pallas_call(
        beside_kernel, out_shape=jax.ShapeDtypeStruct((rows, 2 * width), left.dtype)
    )(left, right)


def paired_body(queries, keys, values, lengths, out_weight):
    rows, width = queries.shape
    axes = ("tok", "head")
    sizes = count, heads = (lax.axis_size("tok"), lax.axis_size("head"))
    tok, head = lax.axis_index("tok"), lax.axis_index("head")
    side, level = tok % 2, tok // 2
    parity, core, half = level % 2, head % 2, head // 2
    send = functools.partial(moved, axes=axes, sizes=sizes)

    own = beside(keys, values)
    back2 = send(own, where=lambda t, h: (t + 2, h) if t + 2 < count else None)
    weight_side = send(out_weight, where=lambda t, h: (t ^ 1, h))
    weight_down = send(out_weight, where=lambda t, h: (t - 4, h) if t >= 4 else None)
    back4 = send(back2, where=lambda t, h: (t + 2, h) if 2 <= t < count - 2 else None)
    back2_side = send(back2, where=lambda t, h: (t ^ 1, h) if t >= 2 else None)
    rest = jnp.where(side == 0, own, back4)
    rest = send(rest, where=lambda t, h: (t ^ 1, h) if t % 2 == 0 or t >= 4 else None)
    late, _ = lax.optimization_barrier((out_weight, back2))
    weight_up = send(late, where=lambda t, h: (t + 4, h) if t in (2, 3) else None)
    later, _ = lax.optimization_barrier((out_weight, back2_side))
    weight_up2 = send(later, where=lambda t, h: (t + 4, h) if t < 2 else None)
    wide = out_weight.shape[1] // 2
    weight_far, weight_far_side = [], []
    for c in (slice(0, wide), slice(wide, None)):
        part = jnp.where(
            level < 2, weight_down[:, c], jnp.where(level == 2, weight_up2[:, c], weight_up[:, c])
        )
        weight_far.append(part)
        weight_far_side.append(send(part, where=lambda t, h: (t ^ 1, h)))

    qpos = tok * rows + jnp.arange(rows, dtype=jnp.int32)
    start = doc_starts(lengths, qpos)[:, None]
    shift = lambda k: (tok - k) * rows
    first = jnp.stack([shift(0), shift(2)])
    second = jnp.stack([shift(2) + rows * (1 - 2 * side), shift(4)])
    third = jnp.where(side == 0, shift(3), shift(1))[None]
    state = attend(queries, start, [own, back2], first, True, None, False)
    state = attend(queries, start, [back2_side, back4], second, False, state, False)
    attn = attend(queries, start, [rest], third, False, state, True, (weight_side,))
    attn_pair = send(attn, where=lambda t, h: (t ^ 2, h))

    mine = core == parity
    keep_rows = jnp.where(mine, attn, attn_pair)
    send_rows = jnp.where(mine, attn_pair, attn)

    def unit(weight, far_off):
        keeper = lambda t: (t // 4) ^ (1 if far_off else 0)
        def product(lines):
            parts = [jnp.dot(lines, w, preferred_element_type=jnp.float32) for w in weight]
            return parts[0] if len(parts) == 1 else jnp.concatenate(parts, axis=1)

        keep = product(keep_rows)
        away = product(send_rows).astype(jnp.bfloat16)
        summed = keep + send(away, where=lambda t, h: (t, h ^ 1))
        low = summed.astype(jnp.bfloat16)
        got = send(low, where=lambda t, h: (t, h ^ 2) if (h // 2) != keeper(t) else None)
        total = (summed + got).astype(jnp.bfloat16)
        over = send(
            total,
            where=lambda t, h: (t ^ 2, h ^ 1)
            if (h // 2) == keeper(t) and (h % 2) != (t // 2) % 2
            else None,
        )
        return jnp.where(mine, total, over)

    far_same = unit(weight_far, True)
    near_same = unit([out_weight], False)
    near_side = unit([weight_side], False)
    far_side = [unit([w], True) for w in weight_far_side]
    far_side = jnp.concatenate(far_side, axis=1)
    is_near = half == level // 2
    same = jnp.where(is_near, near_same, far_same)
    other = jnp.where(is_near, near_side, far_side)
    return jnp.where(
        side == 0,
        jnp.concatenate([same, other], axis=1),
        jnp.concatenate([other, same], axis=1),
    )


def ring_body(queries, keys, values, lengths, out_weight):
    rows = queries.shape[0]
    count = lax.axis_size("tok")
    tok = lax.axis_index("tok")
    qpos = tok * rows + jnp.arange(rows, dtype=jnp.int32)
    start = doc_starts(lengths, qpos)[:, None]
    piece = jnp.concatenate([keys, values], axis=1)
    state = attend(queries, start, [piece], (tok * rows)[None], True, None, False)

    def advance(step, carried):
        piece, state = carried
        piece = lax.ppermute(piece, "tok", [(i, i + 1) for i in range(count - 1)])
        state = attend(queries, start, [piece], ((tok - step) * rows)[None], False, state, False)
        return piece, state

    piece, (acc, _) = lax.fori_loop(1, count // 2 + 1, advance, (piece, state))
    acc = acc.reshape(rows, -1, 2, HD)
    attn = (acc[:, :, 0] / acc[:, :, 1]).reshape(rows, -1).astype(jnp.bfloat16)
    terms = jnp.dot(
        attn,
        lax.all_gather(out_weight, "tok", axis=1, tiled=True),
        preferred_element_type=jnp.float32,
    )
    return lax.psum_scatter(terms.astype(jnp.bfloat16), "head", scatter_dimension=1, tiled=True)


def solution(mesh):
    count, heads = mesh.shape["tok"], mesh.shape["head"]
    body = paired_body if (count, heads) == (8, 4) else ring_body
    placed = (P("tok", "head"), P("tok", "head"), P("tok", "head"), P(), P("head", "tok"))
    return jax.shard_map(
        body, mesh=mesh, in_specs=placed, out_specs=P("tok", "head"), check_vma=False
    )
```
